32 devices in a mesh: row: 4 (over x, core), col: 8 (over z, y).
Axes of the slice: x: 2, y: 2, z: 4, core: 2. Of those that a mesh axis runs over, the one named last changes fastest.
Arguments:
- word_vecs: bfloat16 [32, 4, 1024, 256], P('col', 'row'), may hold values from -1.5 to 1.5
- ctx_vecs: bfloat16 [16, 8, 1024, 256], P('row', 'col'), may hold values from -1.5 to 1.5
- tile_rows: int32 [4, 8, 4], P('row'), may hold values from 0 to 31, as said below
- tile_cols: int32 [4, 8, 4], P(None, 'col'), may hold values from 0 to 15, as said below
- tile_count: int32 [4, 8], replicated, may hold values from 3 to 4
- counts: bfloat16 [4, 8, 4, 1024, 1024], P('row', 'col'), may hold values from 0 to 64
- row_sums: int32 [4, 8, 4, 1024], P('row', 'col'), may hold values from 2000 to 19999
- col_sums: int32 [4, 8, 4, 1024], P('row', 'col'), may hold values from 2000 to 19999
Outputs:
- new_words: bfloat16 [32, 4, 1024, 256], P('col', 'row')
- new_contexts: bfloat16 [16, 8, 1024, 256], P('row', 'col')
The draws below stay inside these ranges and needn't reach their ends.
Inputs may be any that keep to these rules, and one draw needn't show every extreme that they name: On one device (r, c), the values tile_rows[r, c, t] // 4 of its 4 slots are all different. On one device (r, c), the values tile_cols[r, c, t] // 4 of its 4 slots are all different.
All inputs are finite; a program needn't handle non-finite values.
Results may differ from the reference program's by a relative error of at most 0.0032.
Values may be sent and summed in bfloat16 or wider, within the bound.
No kernel may reach another device: no remote copies, remote signals or barrier semaphores. Data moves between devices by JAX's collectives and lax.ppermute only.
A program may use at most 192 MiB of HBM per device.

```python
import jax
import jax.numpy as jnp
from jax import lax

D = 256
BLOCK = 1024
BLK_DEV = 4
TMAX = 4
NBLK_R = 32
NBLK_C = 16
N_ROW = 4
N_COL = 8


def distinct_owners(key, owners, choices):
    key_perm, key_local = jax.random.split(key)
    keys = jax.random.split(key_perm, N_ROW * N_COL)
    picked = jax.vmap(lambda one: jax.random.permutation(one, owners)[:TMAX])(keys)
    picked = picked.reshape(N_ROW, N_COL, TMAX).astype(jnp.int32)
    local = jax.random.randint(key_local, (N_ROW, N_COL, TMAX), 0, choices).astype(jnp.int32)
    return picked * choices + local


def draw_tile_rows(key, part):
    key = jax.random.fold_in(key, 11)
    return distinct_owners(key, N_COL, BLK_DEV)


def draw_tile_cols(key, part):
    key = jax.random.fold_in(key, 23)
    return distinct_owners(key, N_ROW, BLK_DEV)


def draw_tile_count(key, part):
    key = jax.random.fold_in(key, 37)
    key_count, key_spot = jax.random.split(key)
    least = 3 * TMAX // 4
    drawn = jax.random.randint(key_count, (N_ROW * N_COL,), least, TMAX + 1).astype(jnp.int32)
    spot = jax.random.randint(key_spot, (), 0, N_ROW * N_COL - 1)
    drawn = drawn.at[spot].set(TMAX)
    drawn = drawn.at[spot + 1].set(least)
    return drawn.reshape(N_ROW, N_COL)


def draw_counts(key, part):
    key = jax.random.fold_in(key, 41)
    key_zero, key_value = jax.random.split(key)
    shape = (N_ROW, N_COL, TMAX, BLOCK, BLOCK)
    empty = jax.random.randint(key_zero, shape, 0, 5) < 2
    value = jax.random.randint(key_value, shape, 1, 65)
    return jnp.where(empty, 0, value).astype(jnp.float32).astype(jnp.bfloat16)


def place_ends(values, stream_key, smallest, top_value):
    dims = values.shape
    index_at = [jax.random.randint(jax.random.fold_in(stream_key, axis), (), 0, dims[axis]) for axis in range(len(dims))]
    values = values.at[tuple(index_at)].set(smallest)
    longest = dims.index(max(dims))
    index_at[longest] = (index_at[longest] + 1) % dims[longest]
    return values.at[tuple(index_at)].set(top_value)


def steps_of(own_key, dims, pieces, low, high):
    level = 1.0
    for axis_at, parts in pieces:
        heights = jax.random.uniform(jax.random.fold_in(jax.random.fold_in(own_key, 6), axis_at), (parts,), jnp.float32, low / len(pieces), high / len(pieces))
        level = level * jnp.repeat(jnp.exp(heights), dims[axis_at] // parts).reshape((-1,) + (1,) * (len(dims) - 1 - axis_at))
    return level


def bell_draw(rng, shape, scale, bound, pieces=(), held_as=jnp.bfloat16):
    array = jax.random.normal(rng, shape, jnp.float32) * scale
    if len(pieces) > 0:
        array = steps_of(rng, shape, pieces, -0.22, 0.18) * array
    return jnp.clip(array, min=-bound, max=bound).astype(held_as)


def setup_inputs(seed: int = 0) -> dict:
    streams_of = jax.random.split(jax.random.key(seed), 9)
    return {
        "word_vecs": bell_draw(streams_of[0], (NBLK_R, N_ROW, BLOCK, D), 0.25, 1.5, ((0, 8), (1, 4))),
        "ctx_vecs": bell_draw(streams_of[1], (NBLK_C, N_COL, BLOCK, D), 0.25, 1.5, ((0, 4), (1, 8))),
        "tile_rows": draw_tile_rows(jax.random.fold_in(streams_of[8], 71), 0),
        "tile_cols": draw_tile_cols(jax.random.fold_in(streams_of[8], 71), 0),
        "tile_count": draw_tile_count(jax.random.fold_in(streams_of[8], 71), 0),
        "counts": draw_counts(jax.random.fold_in(streams_of[8], 71), 0),
        "row_sums": place_ends(jax.random.randint(streams_of[6], (N_ROW, N_COL, TMAX, BLOCK), 2000, 20000), jax.random.fold_in(streams_of[6], 1), 2000, 19999).astype(jnp.int32),
        "col_sums": place_ends(jax.random.randint(streams_of[7], (N_ROW, N_COL, TMAX, BLOCK), 2000, 20000), jax.random.fold_in(streams_of[7], 1), 2000, 19999).astype(jnp.int32),
    }


shift_term = 16.0
learn_rate = 0.005

def tile_parts(w_tile, c_tile, count_tile, row_total, col_total, keep):
    scores = jnp.dot(w_tile, c_tile.T, preferred_element_type=jnp.float32)
    occur = count_tile.astype(jnp.float32)
    target = jnp.log(jnp.maximum(occur, 1.0)) + shift_term - jnp.log(row_total.astype(jnp.float32))[:, None] - jnp.log(col_total.astype(jnp.float32))[None, :]
    diff = scores - target
    slope = jnp.where(occur > 0, (0.1 + 0.25 * jnp.sqrt(occur)) * diff, jax.nn.sigmoid(diff))
    slope = jnp.where(keep, slope, jnp.zeros_like(slope)).astype(jnp.bfloat16)
    word_part = jnp.dot(slope, c_tile, preferred_element_type=jnp.float32).astype(jnp.bfloat16)
    ctx_part = jnp.dot(slope.T, w_tile, preferred_element_type=jnp.float32).astype(jnp.bfloat16)
    return (word_part, ctx_part)

def widen(part):
    return lax.optimization_barrier(part).astype(jnp.float32)

def reference(word_vecs, ctx_vecs, tile_rows, tile_cols, tile_count, counts, row_sums, col_sums):
    start_words = jnp.zeros(word_vecs.shape, jnp.float32)
    start_contexts = jnp.zeros(ctx_vecs.shape, jnp.float32)

    def visit(carry, device):
        word_grad, ctx_grad = carry
        row_owner = device // N_COL
        col_owner = device % N_COL
        live_tiles = tile_count[row_owner, col_owner]
        for slot in range(TMAX):
            row_block = tile_rows[row_owner, col_owner, slot]
            col_block = tile_cols[row_owner, col_owner, slot]
            w_tile = word_vecs[row_block, row_owner]
            c_tile = ctx_vecs[col_block, col_owner]
            word_part, ctx_part = tile_parts(w_tile, c_tile, counts[row_owner, col_owner, slot], row_sums[row_owner, col_owner, slot], col_sums[row_owner, col_owner, slot], slot < live_tiles)
            word_grad = word_grad.at[row_block, row_owner].add(widen(word_part))
            ctx_grad = ctx_grad.at[col_block, col_owner].add(widen(ctx_part))
        return ((word_grad, ctx_grad), None)
    devices = jnp.arange(N_ROW * N_COL, dtype=jnp.int32)
    (word_grad, ctx_grad), _ = lax.scan(visit, (start_words, start_contexts), devices)
    new_words = (word_vecs.astype(jnp.float32) - learn_rate * word_grad).astype(jnp.bfloat16)
    new_contexts = (ctx_vecs.astype(jnp.float32) - learn_rate * ctx_grad).astype(jnp.bfloat16)
    return (new_words, new_contexts)
```

```python
import functools

import jax
import jax.numpy as jnp
from jax import lax
from jax.experimental import pallas as pl
from jax.experimental.pallas import tpu as pltpu
from jax.sharding import PartitionSpec as P

shift_term = 16.0
learn_rate = 0.005
chunks = 2
bf16, f32, i32 = jnp.bfloat16, jnp.float32, jnp.int32
ANY = pl.BlockSpec(memory_space=pl.ANY)
SMEM = pl.BlockSpec(memory_space=pltpu.SMEM)
VMEM = pl.BlockSpec(memory_space=pltpu.VMEM)
big = pltpu.CompilerParams(vmem_limit_bytes=40 * 1024 * 1024)


def swap(x, axis, shift):
    size = lax.axis_size(axis)
    return lax.ppermute(x, axis, [(i, i ^ shift) for i in range(size)])


def bits_set(v):
    srl = lax.shift_right_logical
    v = v - (srl(v, 1) & 0x55555555)
    v = (v & 0x33333333) + (srl(v, 2) & 0x33333333)
    v = (v + srl(v, 4)) & 0x0F0F0F0F
    return srl(v * 0x01010101, 24)


class Sizes:
    def __init__(self, word_vecs, counts):
        self.cols = lax.axis_size("col")
        self.rows = lax.axis_size("row")
        self.half = self.cols // 2
        self.blocks = word_vecs.shape[0]
        self.block, self.dim = word_vecs.shape[2:]
        self.slots = counts.shape[2]
        self.pool = self.half * self.blocks
        self.part = self.block // self.half
        self.step = self.part // chunks
        self.at_send = 8
        self.at_rank = self.at_send + self.pool
        self.at_fetch = self.at_rank + self.pool
        self.at_live = self.at_fetch + self.half * self.slots
        self.table = self.at_live + self.half * self.slots


def table_kernel(z, me_ref, lists_ref, count_ref, out_ref):
    own_row, own_col = me_ref[0], me_ref[1]
    size = z.pool

    def named_across(s):
        row = own_row ^ s

        def visit(c, masks):
            low, high = masks
            for t in range(z.slots):
                a = lists_ref[s, c * z.slots + t]
                side = (a >= size).astype(i32)
                use = jnp.logical_and(t < count_ref[row, c], side != (c >= z.half).astype(i32))
                bit = jnp.where(use, jnp.int32(1) << (a - side * size), 0)
                low = low | jnp.where(side == 0, bit, 0)
                high = high | jnp.where(side == 1, bit, 0)
            return (low, high)

        return lax.fori_loop(0, z.cols, visit, (jnp.int32(0), jnp.int32(0)))

    low, high = named_across(0)

    def most(s, top):
        a, b = named_across(s)
        return jnp.maximum(top, jnp.maximum(bits_set(a), bits_set(b)))

    out_ref[0] = lax.fori_loop(
        1, z.rows, most, jnp.maximum(bits_set(low), bits_set(high))
    )
    side = (own_col >= z.half).astype(i32)
    place = own_col - side * z.half
    out_mask = jnp.where(side == 0, low, high)
    in_mask = jnp.where(side == 0, high, low)
    turn = place * z.blocks

    def clear(p, none):
        out_ref[z.at_send + p] = 0
        return none

    lax.fori_loop(0, size, clear, 0)

    def rank(p, none):
        bit = jnp.int32(1) << p
        r = bits_set(out_mask & (bit - 1))
        used = (out_mask & bit) != 0
        out_ref[z.at_rank + (p ^ turn)] = jnp.where(used, r, -1)

        @pl.when(used)
        def _():
            out_ref[z.at_send + r] = p ^ turn

        return none

    lax.fori_loop(0, size, rank, 0)

    def fetch(s, none):
        c = side * z.half + (place ^ s)
        for t in range(z.slots):
            a = lists_ref[0, c * z.slots + t]
            there = (a >= size).astype(i32)
            p = a - there * size
            live = t < count_ref[own_row, c]
            lane = size + bits_set(in_mask & ((jnp.int32(1) << p) - 1))
            spot = jnp.where(there == side, p ^ turn, lane)
            out_ref[z.at_fetch + s * z.slots + t] = jnp.where(live, spot, 0)
            out_ref[z.at_live + s * z.slots + t] = live.astype(i32)
        return none

    lax.fori_loop(0, z.half, fetch, 0)


def make_table(z, me, lists, tile_count):
    return pl.pallas_call(
        functools.partial(table_kernel, z),
        out_shape=jax.ShapeDtypeStruct((z.table,), i32),
        in_specs=[SMEM] * 3,
        out_specs=SMEM,
        name="tables",
    )(me, lists, tile_count)


def start_pick(sources, size, spot, target, sem):
    for s, source in enumerate(sources):
        @pl.when(jnp.logical_and(spot >= s * size, spot < (s + 1) * size))
        def _(s=s, source=source):
            pltpu.make_async_copy(source.at[spot - s * size], target, sem).start()


def lanes_kernel(z, cap, table_ref, *refs):
    pool, out_ref, sem = refs[: z.half], refs[-2], refs[-1]
    for j in range(cap):
        start_pick(pool, z.blocks, table_ref[z.at_send + j], out_ref.at[j], sem.at[j])
    for j in range(cap):
        pltpu.make_async_copy(pool[0].at[0], out_ref.at[j], sem.at[j]).wait()


def pick_lanes(z, cap, table, pool, after):
    return pl.pallas_call(
        functools.partial(lanes_kernel, z, cap),
        out_shape=jax.ShapeDtypeStruct((cap, z.step, z.dim), bf16),
        in_specs=[SMEM] + [ANY] * (z.half + len(after)),
        out_specs=VMEM,
        scratch_shapes=[pltpu.SemaphoreType.DMA((cap,))],
        name="pick_lanes",
    )(table, *pool, *after)


def asked_kernel(z, cap, table_ref, *refs):
    pool, lanes = refs[: z.half], refs[z.half]
    outs, sem = refs[z.half + 1 : 2 * z.half + 1], refs[2 * z.half + 1]
    for s in range(z.half):
        for t in range(z.slots):
            n = s * z.slots + t
            spot = table_ref[z.at_fetch + n]
            start_pick(pool, z.blocks, spot, outs[s].at[t], sem.at[n])

            @pl.when(spot >= z.pool)
            def _():
                pltpu.make_async_copy(lanes.at[spot - z.pool], outs[s].at[t], sem.at[n]).start()

    for s in range(z.half):
        for t in range(z.slots):
            pltpu.make_async_copy(pool[0].at[0], outs[s].at[t], sem.at[s * z.slots + t]).wait()


def pick_asked(z, cap, table, pool, lanes):
    return pl.pallas_call(
        functools.partial(asked_kernel, z, cap),
        out_shape=[jax.ShapeDtypeStruct((z.slots, z.step, z.dim), bf16)] * z.half,
        in_specs=[SMEM] + [ANY] * (z.half + 1),
        out_specs=[VMEM] * z.half,
        scratch_shapes=[pltpu.SemaphoreType.DMA((z.half * z.slots,))],
        name="pick_asked",
    )(table, *pool, lanes)


def tile_kernel(z, first, last, info_ref, *refs):
    h = z.half
    words, refs = refs[:h], refs[h:]
    counts, refs = refs[:h], refs[h:]
    row_refs, refs = refs[:h], refs[h:]
    ctx_ref, col_ref, refs = refs[0], refs[1], refs[2:]
    if not first:
        so_far_ref, refs = refs[0], refs[1:]
    parts, refs = refs[:h], refs[h:]
    total_ref, w_ref, scores_ref, slope_ref = refs
    t = pl.program_id(0)
    n = z.step
    live = t < info_ref[0]

    @pl.when(jnp.logical_not(live))
    def _():
        total_ref[...] = jnp.zeros_like(total_ref)

    @pl.when(live)
    def _():
        c_tile = ctx_ref[0]
        col_term = jnp.log(col_ref[0].astype(f32)) - shift_term
        for s in range(h):
            w_ref[s * n : (s + 1) * n, :] = words[s][0]
        for s in range(h):
            rows = slice(s * n, (s + 1) * n)
            scores_ref[rows, :] = lax.dot_general(
                w_ref[rows, :], c_tile, (((1,), (1,)), ((), ())), preferred_element_type=f32
            )
            row_term = jnp.log(row_refs[s][0, 0].astype(f32))
            tall = jnp.transpose(jnp.broadcast_to(row_term, (128, n)))
            strip = 16
            for i in range(n // strip):
                at = s * n + i * strip
                occur = counts[s][0, i * strip : (i + 1) * strip, :].astype(f32)
                least = jnp.maximum(occur, 1.0)
                diff = scores_ref[at : at + strip, :] + col_term + tall[i * strip : (i + 1) * strip, :1]
                diff = diff - jnp.log(least)
                seen = (0.1 + 0.25 * (least * lax.rsqrt(least))) * diff
                unseen = 0.5 * jnp.tanh(0.5 * diff) + 0.5
                slope_ref[at : at + strip, :] = jnp.where(occur > 0, seen, unseen).astype(bf16)
        word_part = jnp.dot(slope_ref[...], c_tile, preferred_element_type=f32).astype(bf16)
        for s in range(h):
            parts[s][0] = word_part[s * n : (s + 1) * n]
        turned = lax.dot_general(
            w_ref[...], slope_ref[...], (((0,), (0,)), ((), ())), preferred_element_type=f32
        )
        if not first:
            turned = turned + so_far_ref[0]
        if last:
            total_ref[0] = jnp.transpose(turned).astype(bf16)
        else:
            total_ref[0] = turned


def tile_step(z, k, info, words, counts, row_sums, col_sums, ctx_tiles, so_far):
    first, last = so_far is None, k == chunks - 1
    h, n = z.half, z.step
    wide = (1, z.dim, z.block)
    tall = (1, z.block, z.dim)

    def counts_spec(s):
        return pl.BlockSpec((1, n, z.block), lambda t, info: (t, info[8 + s] * chunks + k, 0))

    def rows_spec(s):
        return pl.BlockSpec((1, 1, 1, n), lambda t, info: (t, info[8 + s] * chunks + k, 0, 0))

    word_spec = pl.BlockSpec((1, n, z.dim), lambda t, info: (t, 0, 0))
    by_owner = lambda t, info: (info[8 + h + t], 0, 0)
    by_slot = lambda t, info: (t, 0, 0)
    in_specs = [word_spec] * h
    in_specs += [counts_spec(s) for s in range(h)]
    in_specs += [rows_spec(s) for s in range(h)]
    in_specs += [pl.BlockSpec(tall, by_owner), pl.BlockSpec((1, 1, z.block), by_slot)]
    args = [*words, *([counts] * h), *([row_sums] * h), ctx_tiles, col_sums]
    if not first:
        in_specs.append(pl.BlockSpec(wide, by_slot))
        args.append(so_far)
    if last:
        total_shape = jax.ShapeDtypeStruct((z.slots, z.block, z.dim), bf16)
        total_spec = pl.BlockSpec(tall, by_owner)
    else:
        total_shape = jax.ShapeDtypeStruct((z.slots, z.dim, z.block), f32)
        total_spec = pl.BlockSpec(wide, by_slot)
    flops = 6 * z.slots * h * n * z.block * z.dim
    return pl.pallas_call(
        functools.partial(tile_kernel, z, first, last),
        out_shape=[jax.ShapeDtypeStruct((z.slots, n, z.dim), bf16)] * h + [total_shape],
        grid_spec=pltpu.PrefetchScalarGridSpec(
            num_scalar_prefetch=1,
            grid=(z.slots,),
            in_specs=in_specs,
            out_specs=[word_spec] * h + [total_spec],
            scratch_shapes=[
                pltpu.VMEM((h * n, z.dim), bf16),
                pltpu.VMEM((h * n, z.block), f32),
                pltpu.VMEM((h * n, z.block), bf16),
            ],
        ),
        compiler_params=big,
        name="tile_step",
    )(info, *args)


def gather_kernel(z, cap, table_ref, *refs):
    h = z.half
    parts, (own_ref, lanes_ref, total) = refs[:h], refs[-3:]
    total[...] = jnp.zeros_like(total)
    for s in range(h):
        for t in range(z.slots):
            n = s * z.slots + t
            @pl.when(table_ref[z.at_live + n] != 0)
            def _(s=s, t=t, n=n):
                spot = table_ref[z.at_fetch + n]
                total[spot] = total[spot] + parts[s][t].astype(f32)
    own_ref[...] = total[: z.pool]
    lanes_ref[...] = total[z.pool :].astype(bf16)


def sum_parts(z, cap, table, parts, after):
    n = z.step
    return pl.pallas_call(
        functools.partial(gather_kernel, z, cap),
        out_shape=[
            jax.ShapeDtypeStruct((z.pool, n, z.dim), f32),
            jax.ShapeDtypeStruct((cap, n, z.dim), bf16),
        ],
        in_specs=[SMEM] + [VMEM] * z.half + [ANY] * len(after),
        out_specs=[VMEM, VMEM],
        scratch_shapes=[pltpu.VMEM((z.pool + cap, n, z.dim), f32)],
        compiler_params=big,
        name="sum_parts",
    )(table, *parts, *after)


def word_kernel(z, table_ref, own_ref, lanes_ref, *refs):
    pool, outs = refs[: z.half], refs[z.half :]
    for p in range(z.pool):
        s, b = p // z.blocks, p % z.blocks
        rank = table_ref[z.at_rank + p]
        extra = lanes_ref[jnp.maximum(rank, 0)].astype(f32)
        grad = own_ref[p] + jnp.where(rank >= 0, extra, jnp.zeros_like(extra))
        outs[s][b] = (pool[s][b].astype(f32) - learn_rate * grad).astype(bf16)


def word_step(z, table, own, lanes, pool):
    return pl.pallas_call(
        functools.partial(word_kernel, z),
        out_shape=[jax.ShapeDtypeStruct((z.blocks, z.step, z.dim), bf16)] * z.half,
        in_specs=[SMEM] + [VMEM] * (2 + z.half),
        out_specs=[VMEM] * z.half,
        compiler_params=big,
        name="word_step",
    )(table, own, lanes, *pool)


def join_kernel(z, me_ref, *refs):
    pieces, out_ref, sem = refs[:-2], refs[-2], refs[-1]
    place = lax.rem(me_ref[1], z.half)
    copies = []
    for n, piece in enumerate(pieces):
        k, s = n // z.half, n % z.half
        row = pl.multiple_of((place ^ s) * z.part + k * z.step, 16)
        copies.append(pltpu.make_async_copy(piece, out_ref.at[:, pl.ds(row, z.step)], sem.at[n]))
    for copy in copies:
        copy.start()
    for copy in copies:
        copy.wait()


def join_words(z, me, pieces):
    return pl.pallas_call(
        functools.partial(join_kernel, z),
        out_shape=jax.ShapeDtypeStruct((z.blocks, z.block, z.dim), bf16),
        in_specs=[SMEM] + [ANY] * len(pieces),
        out_specs=VMEM,
        scratch_shapes=[pltpu.SemaphoreType.DMA((len(pieces),))],
        name="join_words",
    )(me, *pieces)


def give_kernel(z, info_ref, ctx_ref, out_ref, sem):
    copies = []
    for p in range(z.rows):
        b = info_ref[8 + z.half + z.slots + p]
        copies.append(pltpu.make_async_copy(ctx_ref.at[b], out_ref.at[p], sem.at[p]))
    for copy in copies:
        copy.start()
    for copy in copies:
        copy.wait()


def give_contexts(z, info, contexts):
    return pl.pallas_call(
        functools.partial(give_kernel, z),
        out_shape=jax.ShapeDtypeStruct((z.rows, z.block, z.dim), bf16),
        in_specs=[SMEM, ANY],
        out_specs=VMEM,
        scratch_shapes=[pltpu.SemaphoreType.DMA((z.rows,))],
        name="give_contexts",
    )(info, contexts)


def context_kernel(z, info_ref, back_ref, ctx_ref, out_ref, total):
    total[...] = jnp.zeros_like(total)
    for p in range(z.rows):
        b = info_ref[8 + z.half + z.slots + p]
        total[b] = total[b] + back_ref[p].astype(f32)
    out_ref[...] = (ctx_ref[...].astype(f32) - learn_rate * total[...]).astype(bf16)


def context_step(z, info, back, contexts):
    n = z.block // 4
    return pl.pallas_call(
        functools.partial(context_kernel, z),
        out_shape=jax.ShapeDtypeStruct((z.blocks, z.block, z.dim), bf16),
        grid_spec=pltpu.PrefetchScalarGridSpec(
            num_scalar_prefetch=1,
            grid=(4,),
            in_specs=[
                pl.BlockSpec((z.rows, n, z.dim), lambda i, info: (0, i, 0)),
                pl.BlockSpec((z.blocks, n, z.dim), lambda i, info: (0, i, 0)),
            ],
            out_specs=pl.BlockSpec((z.blocks, n, z.dim), lambda i, info: (0, i, 0)),
            scratch_shapes=[pltpu.VMEM((z.blocks, n, z.dim), f32)],
        ),
        compiler_params=big,
        name="context_step",
    )(info, back, contexts)


def local(word_vecs, ctx_vecs, tile_rows, tile_cols, tile_count, counts, row_sums, col_sums):
    z = Sizes(word_vecs, counts)
    own_row, own_col = lax.axis_index("row"), lax.axis_index("col")
    place = own_col % z.half
    words = word_vecs[:, 0].reshape(z.blocks, z.half, chunks, z.step, z.dim)
    contexts = ctx_vecs[:, 0]
    counts = counts[0, 0]
    row_sums = row_sums[0, 0].reshape(z.slots, z.half * chunks, 1, z.step)
    col_sums = col_sums[0, 0].reshape(z.slots, 1, z.block)
    me = jnp.stack([own_row, own_col]).astype(i32)

    def spread(k):
        pieces = [lax.dynamic_index_in_dim(words[:, :, k], place ^ s, 1, False) for s in range(z.half)]
        return [pieces[0]] + [swap(pieces[s], "col", s) for s in range(1, z.half)]

    flat = tile_rows.reshape(1, z.cols * z.slots)
    lists = jnp.concatenate([flat] + [swap(flat, "row", s) for s in range(1, z.rows)])
    pools = [spread(0)]
    table = make_table(z, me, lists, tile_count)

    col_lists = tile_cols[:, 0]
    mine = lax.dynamic_index_in_dim(col_lists, own_row, 0, False)
    live = tile_count[own_row, own_col]
    given = jnp.sum(jnp.where(col_lists // z.blocks == own_row, col_lists % z.blocks, 0), axis=1)
    info = jnp.concatenate(
        [
            jnp.full((8,), live, i32),
            place ^ jnp.arange(z.half, dtype=i32),
            mine // z.blocks,
            given,
        ]
    ).astype(i32)

    def rest(cap):
        def run(pool_0, table):
            pools = [list(pool_0)] + [spread(k) for k in range(1, chunks)]
            outgoing = give_contexts(z, info, contexts)
            ctx_tiles = lax.all_to_all(outgoing, "row", 0, 0, tiled=True)
            so_far, pieces, lanes_in, lanes_back = None, [], [], []
            for k in range(chunks):
                pool = pools[k]
                lanes = pick_lanes(z, cap, table, pool, lanes_in[-1:])
                lanes_in.append(swap(lanes, "col", z.half))
                asked = pick_asked(z, cap, table, pool, lanes_in[-1])
                tiles = [asked[0]] + [swap(asked[s], "col", s) for s in range(1, z.half)]
                *parts, so_far = tile_step(
                    z, k, info, tiles, counts, row_sums, col_sums, ctx_tiles, so_far
                )
                parts = [parts[0]] + [swap(parts[s], "col", s) for s in range(1, z.half)]
                own, lanes = sum_parts(z, cap, table, parts, lanes_back[-1:])
                lanes_back.append(swap(lanes, "col", z.half))
                new = word_step(z, table, own, lanes_back[-1], pool)
                pieces += [new[0]] + [swap(new[s], "col", s) for s in range(1, z.half)]
            back = lax.all_to_all(so_far, "row", 0, 0, tiled=True)
            new_contexts = context_step(z, info, back, contexts)
            return join_words(z, me, pieces), new_contexts

        return run

    caps = sorted({max(1, z.pool * n // 16) for n in (7, 8, 9, 10, 12, 16)})
    level = sum((table[0] > cap).astype(i32) for cap in caps[:-1])
    new_words, new_contexts = lax.switch(level, [rest(cap) for cap in caps], tuple(pools[0]), table)
    return new_words[:, None], new_contexts[:, None]


def solution(mesh):
    placed = (
        P("col", "row", None, None),
        P("row", "col", None, None),
        P("row", None, None),
        P(None, "col", None),
        P(),
        P("row", "col", None, None, None),
        P("row", "col", None, None),
        P("row", "col", None, None),
    )
    return jax.shard_map(
        local,
        mesh=mesh,
        in_specs=placed,
        out_specs=(P("col", "row", None, None), P("row", "col", None, None)),
        check_vma=False,
    )
```

```python
import functools

import jax
import jax.numpy as jnp
from jax import lax
from jax.experimental import pallas as pl
from jax.experimental.pallas import tpu as pltpu
from jax.sharding import PartitionSpec as P

shift_term = 16.0
learn_rate = 0.005
chunks = 2
bf16, f32, i32 = jnp.bfloat16, jnp.float32, jnp.int32
ANY = pl.BlockSpec(memory_space=pl.ANY)
SMEM = pl.BlockSpec(memory_space=pltpu.SMEM)
VMEM = pl.BlockSpec(memory_space=pltpu.VMEM)
big = pltpu.CompilerParams(vmem_limit_bytes=40 * 1024 * 1024)


def swap(x, axis, shift):
    size = lax.axis_size(axis)
    return lax.ppermute(x, axis, [(i, i ^ shift) for i in range(size)])


def bits_set(v):
    srl = lax.shift_right_logical
    v = v - (srl(v, 1) & 0x55555555)
    v = (v & 0x33333333) + (srl(v, 2) & 0x33333333)
    v = (v + srl(v, 4)) & 0x0F0F0F0F
    return srl(v * 0x01010101, 24)


class Sizes:
    def __init__(self, word_vecs, counts):
        self.cols = lax.axis_size("col")
        self.rows = lax.axis_size("row")
        self.half = self.cols // 2
        self.blocks = word_vecs.shape[0]
        self.block, self.dim = word_vecs.shape[2:]
        self.slots = counts.shape[2]
        self.pool = self.half * self.blocks
        self.part = self.block // self.half
        self.step = self.part // chunks
        self.at_send = 8
        self.at_rank = self.at_send + self.pool
        self.at_fetch = self.at_rank + self.pool
        self.at_live = self.at_fetch + self.half * self.slots
        self.table = self.at_live + self.half * self.slots


def table_kernel(z, me_ref, lists_ref, count_ref, out_ref):
    own_row, own_col = me_ref[0], me_ref[1]
    size = z.pool

    def named_across(s):
        row = own_row ^ s

        def visit(c, masks):
            low, high = masks
            for t in range(z.slots):
                a = lists_ref[s, c * z.slots + t]
                side = (a >= size).astype(i32)
                use = jnp.logical_and(t < count_ref[row, c], side != (c >= z.half).astype(i32))
                bit = jnp.where(use, jnp.int32(1) << (a - side * size), 0)
                low = low | jnp.where(side == 0, bit, 0)
                high = high | jnp.where(side == 1, bit, 0)
            return (low, high)

        return lax.fori_loop(0, z.cols, visit, (jnp.int32(0), jnp.int32(0)))

    low, high = named_across(0)

    def most(s, top):
        a, b = named_across(s)
        return jnp.maximum(top, jnp.maximum(bits_set(a), bits_set(b)))

    out_ref[0] = lax.fori_loop(
        1, z.rows, most, jnp.maximum(bits_set(low), bits_set(high))
    )
    side = (own_col >= z.half).astype(i32)
    place = own_col - side * z.half
    out_mask = jnp.where(side == 0, low, high)
    in_mask = jnp.where(side == 0, high, low)
    turn = place * z.blocks

    def clear(p, none):
        out_ref[z.at_send + p] = 0
        return none

    lax.fori_loop(0, size, clear, 0)

    def rank(p, none):
        bit = jnp.int32(1) << p
        r = bits_set(out_mask & (bit - 1))
        used = (out_mask & bit) != 0
        out_ref[z.at_rank + (p ^ turn)] = jnp.where(used, r, -1)

        @pl.when(used)
        def _():
            out_ref[z.at_send + r] = p ^ turn

        return none

    lax.fori_loop(0, size, rank, 0)

    def fetch(s, none):
        c = side * z.half + (place ^ s)
        for t in range(z.slots):
            a = lists_ref[0, c * z.slots + t]
            there = (a >= size).astype(i32)
            p = a - there * size
            live = t < count_ref[own_row, c]
            lane = size + bits_set(in_mask & ((jnp.int32(1) << p) - 1))
            spot = jnp.where(there == side, p ^ turn, lane)
            out_ref[z.at_fetch + s * z.slots + t] = jnp.where(live, spot, 0)
            out_ref[z.at_live + s * z.slots + t] = live.astype(i32)
        return none

    lax.fori_loop(0, z.half, fetch, 0)


def make_table(z, me, lists, tile_count):
    return pl.pallas_call(
        functools.partial(table_kernel, z),
        out_shape=jax.ShapeDtypeStruct((z.table,), i32),
        in_specs=[SMEM] * 3,
        out_specs=SMEM,
        name="tables",
    )(me, lists, tile_count)


def split_kernel(z, k, me_ref, words_ref, *refs):
    outs, sem = refs[-1 - z.half : -1], refs[-1]
    place = lax.rem(me_ref[1], z.half)
    copies = []
    for s in range(z.half):
        row = pl.multiple_of((place ^ s) * z.part + k * z.step, 16)
        copies.append(pltpu.make_async_copy(words_ref.at[:, pl.ds(row, z.step)], outs[s], sem.at[s]))
    for copy in copies:
        copy.start()
    for copy in copies:
        copy.wait()


def split_words(z, k, me, words, after):
    return pl.pallas_call(
        functools.partial(split_kernel, z, k),
        out_shape=[jax.ShapeDtypeStruct((z.blocks, z.step, z.dim), bf16)] * z.half,
        in_specs=[SMEM, ANY] + [ANY] * len(after),
        out_specs=[VMEM] * z.half,
        scratch_shapes=[pltpu.SemaphoreType.DMA((z.half,))],
        name="split_words",
    )(me, words, *after)


def start_pick(sources, size, spot, target, sem):
    for s, source in enumerate(sources):
        @pl.when(jnp.logical_and(spot >= s * size, spot < (s + 1) * size))
        def _(s=s, source=source):
            pltpu.make_async_copy(source.at[spot - s * size], target, sem).start()


def lanes_kernel(z, cap, table_ref, *refs):
    pool, out_ref, sem = refs[: z.half], refs[-2], refs[-1]
    for j in range(cap):
        start_pick(pool, z.blocks, table_ref[z.at_send + j], out_ref.at[j], sem.at[j])
    for j in range(cap):
        pltpu.make_async_copy(pool[0].at[0], out_ref.at[j], sem.at[j]).wait()


def pick_lanes(z, cap, table, pool, after):
    return pl.pallas_call(
        functools.partial(lanes_kernel, z, cap),
        out_shape=jax.ShapeDtypeStruct((cap, z.step, z.dim), bf16),
        in_specs=[SMEM] + [ANY] * (z.half + len(after)),
        out_specs=VMEM,
        scratch_shapes=[pltpu.SemaphoreType.DMA((cap,))],
        name="pick_lanes",
    )(table, *pool, *after)


def asked_kernel(z, cap, table_ref, *refs):
    pool, lanes = refs[: z.half], refs[z.half]
    outs, sem = refs[-1 - z.half : -1], refs[-1]
    for s in range(z.half):
        for t in range(z.slots):
            n = s * z.slots + t
            spot = table_ref[z.at_fetch + n]
            start_pick(pool, z.blocks, spot, outs[s].at[t], sem.at[n])

            @pl.when(spot >= z.pool)
            def _():
                pltpu.make_async_copy(lanes.at[spot - z.pool], outs[s].at[t], sem.at[n]).start()

    for s in range(z.half):
        for t in range(z.slots):
            pltpu.make_async_copy(pool[0].at[0], outs[s].at[t], sem.at[s * z.slots + t]).wait()


def pick_asked(z, cap, table, pool, lanes, after):
    return pl.pallas_call(
        functools.partial(asked_kernel, z, cap),
        out_shape=[jax.ShapeDtypeStruct((z.slots, z.step, z.dim), bf16)] * z.half,
        in_specs=[SMEM] + [ANY] * (z.half + 1 + len(after)),
        out_specs=[VMEM] * z.half,
        scratch_shapes=[pltpu.SemaphoreType.DMA((z.half * z.slots,))],
        name="pick_asked",
    )(table, *pool, lanes, *after)


def tile_kernel(z, first, last, waits, info_ref, *refs):
    h = z.half
    refs = refs[waits:]
    words, refs = refs[:h], refs[h:]
    counts, refs = refs[:h], refs[h:]
    row_refs, refs = refs[:h], refs[h:]
    ctx_ref, col_ref, refs = refs[0], refs[1], refs[2:]
    if not first:
        so_far_ref, refs = refs[0], refs[1:]
    parts, refs = refs[:h], refs[h:]
    total_ref, w_ref, scores_ref, slope_ref = refs
    t = pl.program_id(0)
    n = z.step
    live = t < info_ref[0]

    @pl.when(jnp.logical_not(live))
    def _():
        total_ref[...] = jnp.zeros_like(total_ref)

    @pl.when(live)
    def _():
        c_tile = ctx_ref[0]
        col_term = jnp.log(col_ref[0].astype(f32)) - shift_term
        for s in range(h):
            w_ref[s * n : (s + 1) * n, :] = words[s][0]
        for s in range(h):
            rows = slice(s * n, (s + 1) * n)
            scores_ref[rows, :] = lax.dot_general(
                w_ref[rows, :], c_tile, (((1,), (1,)), ((), ())), preferred_element_type=f32
            )
            row_term = jnp.log(row_refs[s][0, 0].astype(f32))
            tall = jnp.transpose(jnp.broadcast_to(row_term, (128, n)))
            strip = 16
            for i in range(n // strip):
                at = s * n + i * strip
                occur = counts[s][0, i * strip : (i + 1) * strip, :].astype(f32)
                least = jnp.maximum(occur, 1.0)
                diff = scores_ref[at : at + strip, :] + col_term + tall[i * strip : (i + 1) * strip, :1]
                diff = diff - jnp.log(least)
                seen = (0.1 + 0.25 * (least * lax.rsqrt(least))) * diff
                unseen = 0.5 * jnp.tanh(0.5 * diff) + 0.5
                slope_ref[at : at + strip, :] = jnp.where(occur > 0, seen, unseen).astype(bf16)
        word_part = jnp.dot(slope_ref[...], c_tile, preferred_element_type=f32).astype(bf16)
        for s in range(h):
            parts[s][0] = word_part[s * n : (s + 1) * n]
        turned = lax.dot_general(
            w_ref[...], slope_ref[...], (((0,), (0,)), ((), ())), preferred_element_type=f32
        )
        if not first:
            turned = turned + so_far_ref[0]
        if last:
            total_ref[0] = jnp.transpose(turned).astype(bf16)
        else:
            total_ref[0] = turned


def tile_step(z, k, info, words, counts, row_sums, col_sums, ctx_tiles, so_far, after):
    first, last = so_far is None, k == chunks - 1
    h, n = z.half, z.step
    wide = (1, z.dim, z.block)
    tall = (1, z.block, z.dim)

    def counts_spec(s):
        return pl.BlockSpec((1, n, z.block), lambda t, info: (t, info[8 + s] * chunks + k, 0))

    def rows_spec(s):
        return pl.BlockSpec((1, 1, 1, n), lambda t, info: (t, info[8 + s] * chunks + k, 0, 0))

    word_spec = pl.BlockSpec((1, n, z.dim), lambda t, info: (t, 0, 0))
    by_owner = lambda t, info: (info[8 + h + t], 0, 0)
    by_slot = lambda t, info: (t, 0, 0)
    in_specs = [ANY] * len(after) + [word_spec] * h
    in_specs += [counts_spec(s) for s in range(h)]
    in_specs += [rows_spec(s) for s in range(h)]
    in_specs += [pl.BlockSpec(tall, by_owner), pl.BlockSpec((1, 1, z.block), by_slot)]
    args = [*after, *words, *([counts] * h), *([row_sums] * h), ctx_tiles, col_sums]
    if not first:
        in_specs.append(pl.BlockSpec(wide, by_slot))
        args.append(so_far)
    if last:
        total_shape = jax.ShapeDtypeStruct((z.slots, z.block, z.dim), bf16)
        total_spec = pl.BlockSpec(tall, by_owner)
    else:
        total_shape = jax.ShapeDtypeStruct((z.slots, z.dim, z.block), f32)
        total_spec = pl.BlockSpec(wide, by_slot)
    flops = 6 * z.slots * h * n * z.block * z.dim
    return pl.pallas_call(
        functools.partial(tile_kernel, z, first, last, len(after)),
        out_shape=[jax.ShapeDtypeStruct((z.slots, n, z.dim), bf16)] * h + [total_shape],
        grid_spec=pltpu.PrefetchScalarGridSpec(
            num_scalar_prefetch=1,
            grid=(z.slots,),
            in_specs=in_specs,
            out_specs=[word_spec] * h + [total_spec],
            scratch_shapes=[
                pltpu.VMEM((h * n, z.dim), bf16),
                pltpu.VMEM((h * n, z.block), f32),
                pltpu.VMEM((h * n, z.block), bf16),
            ],
        ),
        compiler_params=big,
        name="tile_step",
    )(info, *args)


def gather_kernel(z, cap, table_ref, *refs):
    h = z.half
    parts, (own_ref, lanes_ref, total) = refs[:h], refs[-3:]
    total[...] = jnp.zeros_like(total)
    for s in range(h):
        for t in range(z.slots):
            n = s * z.slots + t
            @pl.when(table_ref[z.at_live + n] != 0)
            def _(s=s, t=t, n=n):
                spot = table_ref[z.at_fetch + n]
                total[spot] = total[spot] + parts[s][t].astype(f32)
    own_ref[...] = total[: z.pool]
    lanes_ref[...] = total[z.pool :].astype(bf16)


def sum_parts(z, cap, table, parts, after):
    n = z.step
    return pl.pallas_call(
        functools.partial(gather_kernel, z, cap),
        out_shape=[
            jax.ShapeDtypeStruct((z.pool, n, z.dim), f32),
            jax.ShapeDtypeStruct((cap, n, z.dim), bf16),
        ],
        in_specs=[SMEM] + [VMEM] * z.half + [ANY] * len(after),
        out_specs=[VMEM, VMEM],
        scratch_shapes=[pltpu.VMEM((z.pool + cap, n, z.dim), f32)],
        compiler_params=big,
        name="sum_parts",
    )(table, *parts, *after)


def word_kernel(z, table_ref, own_ref, lanes_ref, *refs):
    pool, outs = refs[: z.half], refs[z.half :]
    for p in range(z.pool):
        s, b = p // z.blocks, p % z.blocks
        rank = table_ref[z.at_rank + p]
        extra = lanes_ref[jnp.maximum(rank, 0)].astype(f32)
        grad = own_ref[p] + jnp.where(rank >= 0, extra, jnp.zeros_like(extra))
        outs[s][b] = (pool[s][b].astype(f32) - learn_rate * grad).astype(bf16)


def word_step(z, table, own, lanes, pool):
    return pl.pallas_call(
        functools.partial(word_kernel, z),
        out_shape=[jax.ShapeDtypeStruct((z.blocks, z.step, z.dim), bf16)] * z.half,
        in_specs=[SMEM] + [VMEM] * (2 + z.half),
        out_specs=[VMEM] * z.half,
        compiler_params=big,
        name="word_step",
    )(table, own, lanes, *pool)


def join_kernel(z, me_ref, *refs):
    pieces, out_ref, sem = refs[:-2], refs[-2], refs[-1]
    place = lax.rem(me_ref[1], z.half)
    copies = []
    for n, piece in enumerate(pieces):
        k, s = n // z.half, n % z.half
        row = pl.multiple_of((place ^ s) * z.part + k * z.step, 16)
        copies.append(pltpu.make_async_copy(piece, out_ref.at[:, pl.ds(row, z.step)], sem.at[n]))
    for copy in copies:
        copy.start()
    for copy in copies:
        copy.wait()


def join_words(z, me, pieces):
    return pl.pallas_call(
        functools.partial(join_kernel, z),
        out_shape=jax.ShapeDtypeStruct((z.blocks, z.block, z.dim), bf16),
        in_specs=[SMEM] + [ANY] * len(pieces),
        out_specs=VMEM,
        scratch_shapes=[pltpu.SemaphoreType.DMA((len(pieces),))],
        name="join_words",
    )(me, *pieces)


def give_kernel(z, info_ref, ctx_ref, *refs):
    out_ref, sem = refs[-2:]
    copies = []
    for p in range(z.rows):
        b = info_ref[8 + z.half + z.slots + p]
        copies.append(pltpu.make_async_copy(ctx_ref.at[b], out_ref.at[p], sem.at[p]))
    for copy in copies:
        copy.start()
    for copy in copies:
        copy.wait()


def give_contexts(z, info, contexts, after):
    return pl.pallas_call(
        functools.partial(give_kernel, z),
        out_shape=jax.ShapeDtypeStruct((z.rows, z.block, z.dim), bf16),
        in_specs=[SMEM, ANY] + [ANY] * len(after),
        out_specs=VMEM,
        scratch_shapes=[pltpu.SemaphoreType.DMA((z.rows,))],
        name="give_contexts",
    )(info, contexts, *after)


def context_kernel(z, info_ref, back_ref, ctx_ref, out_ref, total):
    total[...] = jnp.zeros_like(total)
    for p in range(z.rows):
        b = info_ref[8 + z.half + z.slots + p]
        total[b] = total[b] + back_ref[p].astype(f32)
    out_ref[...] = (ctx_ref[...].astype(f32) - learn_rate * total[...]).astype(bf16)


def context_step(z, info, back, contexts):
    n = z.block // 4
    return pl.pallas_call(
        functools.partial(context_kernel, z),
        out_shape=jax.ShapeDtypeStruct((z.blocks, z.block, z.dim), bf16),
        grid_spec=pltpu.PrefetchScalarGridSpec(
            num_scalar_prefetch=1,
            grid=(4,),
            in_specs=[
                pl.BlockSpec((z.rows, n, z.dim), lambda i, info: (0, i, 0)),
                pl.BlockSpec((z.blocks, n, z.dim), lambda i, info: (0, i, 0)),
            ],
            out_specs=pl.BlockSpec((z.blocks, n, z.dim), lambda i, info: (0, i, 0)),
            scratch_shapes=[pltpu.VMEM((z.blocks, n, z.dim), f32)],
        ),
        compiler_params=big,
        name="context_step",
    )(info, back, contexts)


def local(word_vecs, ctx_vecs, tile_rows, tile_cols, tile_count, counts, row_sums, col_sums):
    z = Sizes(word_vecs, counts)
    own_row, own_col = lax.axis_index("row"), lax.axis_index("col")
    place = own_col % z.half
    words = word_vecs[:, 0]
    contexts = ctx_vecs[:, 0]
    counts = counts[0, 0]
    row_sums = row_sums[0, 0].reshape(z.slots, z.half * chunks, 1, z.step)
    col_sums = col_sums[0, 0].reshape(z.slots, 1, z.block)
    me = jnp.stack([own_row, own_col]).astype(i32)

    def spread(k, after):
        pieces = split_words(z, k, me, words, after)
        return [pieces[0]] + [swap(pieces[s], "col", s) for s in range(1, z.half)]

    flat = tile_rows.reshape(1, z.cols * z.slots)
    lists = jnp.concatenate([flat] + [swap(flat, "row", s) for s in range(1, z.rows)])
    pool_0 = spread(0, [])
    table = make_table(z, me, lists, tile_count)

    col_lists = tile_cols[:, 0]
    mine = lax.dynamic_index_in_dim(col_lists, own_row, 0, False)
    live = tile_count[own_row, own_col]
    given = jnp.sum(jnp.where(col_lists // z.blocks == own_row, col_lists % z.blocks, 0), axis=1)
    info = jnp.concatenate(
        [
            jnp.full((8,), live, i32),
            place ^ jnp.arange(z.half, dtype=i32),
            mine // z.blocks,
            given,
        ]
    ).astype(i32)

    def exchange(pieces):
        return [pieces[0]] + [swap(pieces[s], "col", s) for s in range(1, z.half)]

    def rest(cap):
        def run(pool_0, table):
            outgoing = give_contexts(z, info, contexts, [])
            ctx_tiles = lax.all_to_all(outgoing, "row", 0, 0, tiled=True)
            pools = [list(pool_0)] + [spread(k, []) for k in range(1, chunks)]
            so_far, lanes, asked, made, own, returned, pieces = None, [], [], [], [], [], []
            for k in range(chunks):
                lanes.append(across_col(pick_lanes(z, cap, table, pools[k], lanes[-1:])))
                order = []
                asked.append(pick_asked(z, cap, table, pools[k], lanes[k], order))
                *out, so_far = tile_step(
                    z, k, info, exchange(asked[k]), counts, row_sums, col_sums, ctx_tiles, so_far, []
                )
                made.append(out)
            for k in range(chunks):
                order = returned[-1:]
                sum_step(k, cap, table, exchange(made[k]), own, returned, order)
                pieces += exchange(word_step(z, table, own[k], returned[k], pools[k]))
            back = lax.all_to_all(so_far, "row", 0, 0, tiled=True)
            new_contexts = context_step(z, info, back, contexts)
            return join_words(z, me, pieces), new_contexts

        def sum_step(k, cap, table, parts, own, returned, after):
            total, grads = sum_parts(z, cap, table, parts, after)
            own.append(total)
            returned.append(across_col(grads))
            return [grads]

        return run

    def across_col(x):
        return swap(x, "col", z.half)

    caps = sorted({max(1, z.pool * n // 16) for n in (9, 16)})
    level = sum((table[0] > cap).astype(i32) for cap in caps[:-1])
    new_words, new_contexts = lax.switch(level, [rest(cap) for cap in caps], tuple(pool_0), table)
    return new_words[:, None], new_contexts[:, None]


def solution(mesh):
    placed = (
        P("col", "row", None, None),
        P("row", "col", None, None),
        P("row", None, None),
        P(None, "col", None),
        P(),
        P("row", "col", None, None, None),
        P("row", "col", None, None),
        P("row", "col", None, None),
    )
    return jax.shard_map(
        local,
        mesh=mesh,
        in_specs=placed,
        out_specs=(P("col", "row", None, None), P("row", "col", None, None)),
        check_vma=False,
    )
```

```python
import functools

import jax
import jax.numpy as jnp
from jax import lax
from jax.experimental import pallas as pl
from jax.experimental.pallas import tpu as pltpu
from jax.sharding import PartitionSpec as P

shift_term = 16.0
learn_rate = 0.005
chunks = 2
bf16, f32, i32 = jnp.bfloat16, jnp.float32, jnp.int32
ANY = pl.BlockSpec(memory_space=pl.ANY)
SMEM = pl.BlockSpec(memory_space=pltpu.SMEM)
VMEM = pl.BlockSpec(memory_space=pltpu.VMEM)
big = pltpu.CompilerParams(vmem_limit_bytes=40 * 1024 * 1024)


def swap(x, axis, shift):
    size = lax.axis_size(axis)
    return lax.ppermute(x, axis, [(i, i ^ shift) for i in range(size)])


def bits_set(v):
    srl = lax.shift_right_logical
    v = v - (srl(v, 1) & 0x55555555)
    v = (v & 0x33333333) + (srl(v, 2) & 0x33333333)
    v = (v + srl(v, 4)) & 0x0F0F0F0F
    return srl(v * 0x01010101, 24)


class Sizes:
    def __init__(self, word_vecs, counts):
        self.cols = lax.axis_size("col")
        self.rows = lax.axis_size("row")
        self.half = self.cols // 2
        self.blocks = word_vecs.shape[0]
        self.block, self.dim = word_vecs.shape[2:]
        self.slots = counts.shape[2]
        self.pool = self.half * self.blocks
        self.part = self.block // self.half
        self.step = self.part // chunks
        self.at_send = 8
        self.at_rank = self.at_send + self.pool
        self.at_fetch = self.at_rank + self.pool
        self.at_live = self.at_fetch + self.half * self.slots
        self.table = self.at_live + self.half * self.slots


def table_kernel(z, me_ref, lists_ref, count_ref, out_ref):
    own_row, own_col = me_ref[0], me_ref[1]
    size = z.pool

    def named_across(s):
        row = own_row ^ s

        def visit(c, masks):
            low, high = masks
            for t in range(z.slots):
                a = lists_ref[s, c * z.slots + t]
                side = (a >= size).astype(i32)
                use = jnp.logical_and(t < count_ref[row, c], side != (c >= z.half).astype(i32))
                bit = jnp.where(use, jnp.int32(1) << (a - side * size), 0)
                low = low | jnp.where(side == 0, bit, 0)
                high = high | jnp.where(side == 1, bit, 0)
            return (low, high)

        return lax.fori_loop(0, z.cols, visit, (jnp.int32(0), jnp.int32(0)))

    low, high = named_across(0)

    def most(s, top):
        a, b = named_across(s)
        return jnp.maximum(top, jnp.maximum(bits_set(a), bits_set(b)))

    out_ref[0] = lax.fori_loop(
        1, z.rows, most, jnp.maximum(bits_set(low), bits_set(high))
    )
    side = (own_col >= z.half).astype(i32)
    place = own_col - side * z.half
    out_mask = jnp.where(side == 0, low, high)
    in_mask = jnp.where(side == 0, high, low)
    turn = place * z.blocks

    def clear(p, none):
        out_ref[z.at_send + p] = 0
        return none

    lax.fori_loop(0, size, clear, 0)

    def rank(p, none):
        bit = jnp.int32(1) << p
        r = bits_set(out_mask & (bit - 1))
        used = (out_mask & bit) != 0
        out_ref[z.at_rank + (p ^ turn)] = jnp.where(used, r, -1)

        @pl.when(used)
        def _():
            out_ref[z.at_send + r] = p ^ turn

        return none

    lax.fori_loop(0, size, rank, 0)

    def fetch(s, none):
        c = side * z.half + (place ^ s)
        for t in range(z.slots):
            a = lists_ref[0, c * z.slots + t]
            there = (a >= size).astype(i32)
            p = a - there * size
            live = t < count_ref[own_row, c]
            lane = size + bits_set(in_mask & ((jnp.int32(1) << p) - 1))
            spot = jnp.where(there == side, p ^ turn, lane)
            out_ref[z.at_fetch + s * z.slots + t] = jnp.where(live, spot, 0)
            out_ref[z.at_live + s * z.slots + t] = live.astype(i32)
        return none

    lax.fori_loop(0, z.half, fetch, 0)


def make_table(z, me, lists, tile_count):
    return pl.pallas_call(
        functools.partial(table_kernel, z),
        out_shape=jax.ShapeDtypeStruct((z.table,), i32),
        in_specs=[SMEM] * 3,
        out_specs=SMEM,
        name="tables",
    )(me, lists, tile_count)


def split_kernel(z, k, me_ref, words_ref, *refs):
    outs, sem = refs[-1 - z.half : -1], refs[-1]
    place = lax.rem(me_ref[1], z.half)
    copies = []
    for s in range(z.half):
        row = pl.multiple_of((place ^ s) * z.part + k * z.step, 16)
        copies.append(pltpu.make_async_copy(words_ref.at[:, pl.ds(row, z.step)], outs[s], sem.at[s]))
    for copy in copies:
        copy.start()
    for copy in copies:
        copy.wait()


def split_words(z, k, me, words, after):
    return pl.pallas_call(
        functools.partial(split_kernel, z, k),
        out_shape=[jax.ShapeDtypeStruct((z.blocks, z.step, z.dim), bf16)] * z.half,
        in_specs=[SMEM, ANY] + [ANY] * len(after),
        out_specs=[VMEM] * z.half,
        scratch_shapes=[pltpu.SemaphoreType.DMA((z.half,))],
        name="split_words",
    )(me, words, *after)


def start_pick(sources, size, spot, target, sem):
    for s, source in enumerate(sources):
        @pl.when(jnp.logical_and(spot >= s * size, spot < (s + 1) * size))
        def _(s=s, source=source):
            pltpu.make_async_copy(source.at[spot - s * size], target, sem).start()


def lanes_kernel(z, cap, table_ref, *refs):
    pool, out_ref, sem = refs[: z.half], refs[-2], refs[-1]
    for j in range(cap):
        start_pick(pool, z.blocks, table_ref[z.at_send + j], out_ref.at[j], sem.at[j])
    for j in range(cap):
        pltpu.make_async_copy(pool[0].at[0], out_ref.at[j], sem.at[j]).wait()


def pick_lanes(z, cap, table, pool, after):
    return pl.pallas_call(
        functools.partial(lanes_kernel, z, cap),
        out_shape=jax.ShapeDtypeStruct((cap, z.step, z.dim), bf16),
        in_specs=[SMEM] + [ANY] * (z.half + len(after)),
        out_specs=VMEM,
        scratch_shapes=[pltpu.SemaphoreType.DMA((cap,))],
        name="pick_lanes",
    )(table, *pool, *after)


def asked_kernel(z, cap, table_ref, *refs):
    pool, lanes = refs[: z.half], refs[z.half]
    outs, sem = refs[-1 - z.half : -1], refs[-1]
    for s in range(z.half):
        for t in range(z.slots):
            n = s * z.slots + t
            spot = table_ref[z.at_fetch + n]
            start_pick(pool, z.blocks, spot, outs[s].at[t], sem.at[n])

            @pl.when(spot >= z.pool)
            def _():
                pltpu.make_async_copy(lanes.at[spot - z.pool], outs[s].at[t], sem.at[n]).start()

    for s in range(z.half):
        for t in range(z.slots):
            pltpu.make_async_copy(pool[0].at[0], outs[s].at[t], sem.at[s * z.slots + t]).wait()


def pick_asked(z, cap, table, pool, lanes, after):
    return pl.pallas_call(
        functools.partial(asked_kernel, z, cap),
        out_shape=[jax.ShapeDtypeStruct((z.slots, z.step, z.dim), bf16)] * z.half,
        in_specs=[SMEM] + [ANY] * (z.half + 1 + len(after)),
        out_specs=[VMEM] * z.half,
        scratch_shapes=[pltpu.SemaphoreType.DMA((z.half * z.slots,))],
        name="pick_asked",
    )(table, *pool, lanes, *after)


def tile_kernel(z, first, last, waits, info_ref, *refs):
    h = z.half
    refs = refs[waits:]
    words, refs = refs[:h], refs[h:]
    counts, refs = refs[:h], refs[h:]
    row_refs, refs = refs[:h], refs[h:]
    ctx_ref, col_ref, refs = refs[0], refs[1], refs[2:]
    if not first:
        so_far_ref, refs = refs[0], refs[1:]
    parts, refs = refs[:h], refs[h:]
    total_ref, w_ref, scores_ref, slope_ref = refs
    t = pl.program_id(0)
    n = z.step
    live = t < info_ref[0]

    @pl.when(jnp.logical_not(live))
    def _():
        total_ref[...] = jnp.zeros_like(total_ref)

    @pl.when(live)
    def _():
        c_tile = ctx_ref[0]
        col_term = jnp.log(col_ref[0].astype(f32)) - shift_term
        for s in range(h):
            w_ref[s * n : (s + 1) * n, :] = words[s][0]
        for s in range(h):
            rows = slice(s * n, (s + 1) * n)
            scores_ref[rows, :] = lax.dot_general(
                w_ref[rows, :], c_tile, (((1,), (1,)), ((), ())), preferred_element_type=f32
            )
            row_term = jnp.log(row_refs[s][0, 0].astype(f32))
            tall = jnp.transpose(jnp.broadcast_to(row_term, (128, n)))
            strip = 16
            for i in range(n // strip):
                at = s * n + i * strip
                occur = counts[s][0, i * strip : (i + 1) * strip, :].astype(f32)
                least = jnp.maximum(occur, 1.0)
                diff = scores_ref[at : at + strip, :] + col_term + tall[i * strip : (i + 1) * strip, :1]
                diff = diff - jnp.log(least)
                seen = (0.1 + 0.25 * (least * lax.rsqrt(least))) * diff
                unseen = 0.5 * jnp.tanh(0.5 * diff) + 0.5
                slope_ref[at : at + strip, :] = jnp.where(occur > 0, seen, unseen).astype(bf16)
        word_part = jnp.dot(slope_ref[...], c_tile, preferred_element_type=f32).astype(bf16)
        for s in range(h):
            parts[s][0] = word_part[s * n : (s + 1) * n]
        turned = lax.dot_general(
            w_ref[...], slope_ref[...], (((0,), (0,)), ((), ())), preferred_element_type=f32
        )
        if not first:
            turned = turned + so_far_ref[0]
        if last:
            total_ref[0] = jnp.transpose(turned).astype(bf16)
        else:
            total_ref[0] = turned


def tile_step(z, k, info, words, counts, row_sums, col_sums, ctx_tiles, so_far, after):
    first, last = so_far is None, k == chunks - 1
    h, n = z.half, z.step
    wide = (1, z.dim, z.block)
    tall = (1, z.block, z.dim)

    def counts_spec(s):
        return pl.BlockSpec((1, n, z.block), lambda t, info: (t, info[8 + s] * chunks + k, 0))

    def rows_spec(s):
        return pl.BlockSpec((1, 1, 1, n), lambda t, info: (t, info[8 + s] * chunks + k, 0, 0))

    word_spec = pl.BlockSpec((1, n, z.dim), lambda t, info: (t, 0, 0))
    by_owner = lambda t, info: (info[8 + h + t], 0, 0)
    by_slot = lambda t, info: (t, 0, 0)
    in_specs = [ANY] * len(after) + [word_spec] * h
    in_specs += [counts_spec(s) for s in range(h)]
    in_specs += [rows_spec(s) for s in range(h)]
    in_specs += [pl.BlockSpec(tall, by_owner), pl.BlockSpec((1, 1, z.block), by_slot)]
    args = [*after, *words, *([counts] * h), *([row_sums] * h), ctx_tiles, col_sums]
    if not first:
        in_specs.append(pl.BlockSpec(wide, by_slot))
        args.append(so_far)
    if last:
        total_shape = jax.ShapeDtypeStruct((z.slots, z.block, z.dim), bf16)
        total_spec = pl.BlockSpec(tall, by_owner)
    else:
        total_shape = jax.ShapeDtypeStruct((z.slots, z.dim, z.block), f32)
        total_spec = pl.BlockSpec(wide, by_slot)
    flops = 6 * z.slots * h * n * z.block * z.dim
    return pl.pallas_call(
        functools.partial(tile_kernel, z, first, last, len(after)),
        out_shape=[jax.ShapeDtypeStruct((z.slots, n, z.dim), bf16)] * h + [total_shape],
        grid_spec=pltpu.PrefetchScalarGridSpec(
            num_scalar_prefetch=1,
            grid=(z.slots,),
            in_specs=in_specs,
            out_specs=[word_spec] * h + [total_spec],
            scratch_shapes=[
                pltpu.VMEM((h * n, z.dim), bf16),
                pltpu.VMEM((h * n, z.block), f32),
                pltpu.VMEM((h * n, z.block), bf16),
            ],
        ),
        compiler_params=big,
        name="tile_step",
    )(info, *args)


def gather_kernel(z, cap, table_ref, *refs):
    h = z.half
    parts, (own_ref, lanes_ref, total) = refs[:h], refs[-3:]
    total[...] = jnp.zeros_like(total)
    for s in range(h):
        for t in range(z.slots):
            n = s * z.slots + t
            @pl.when(table_ref[z.at_live + n] != 0)
            def _(s=s, t=t, n=n):
                spot = table_ref[z.at_fetch + n]
                total[spot] = total[spot] + parts[s][t].astype(f32)
    own_ref[...] = total[: z.pool]
    lanes_ref[...] = total[z.pool :].astype(bf16)


def sum_parts(z, cap, table, parts, after):
    n = z.step
    return pl.pallas_call(
        functools.partial(gather_kernel, z, cap),
        out_shape=[
            jax.ShapeDtypeStruct((z.pool, n, z.dim), f32),
            jax.ShapeDtypeStruct((cap, n, z.dim), bf16),
        ],
        in_specs=[SMEM] + [VMEM] * z.half + [ANY] * len(after),
        out_specs=[VMEM, VMEM],
        scratch_shapes=[pltpu.VMEM((z.pool + cap, n, z.dim), f32)],
        compiler_params=big,
        name="sum_parts",
    )(table, *parts, *after)


def word_kernel(z, table_ref, own_ref, lanes_ref, *refs):
    pool, outs = refs[: z.half], refs[z.half :]
    for p in range(z.pool):
        s, b = p // z.blocks, p % z.blocks
        rank = table_ref[z.at_rank + p]
        extra = lanes_ref[jnp.maximum(rank, 0)].astype(f32)
        grad = own_ref[p] + jnp.where(rank >= 0, extra, jnp.zeros_like(extra))
        outs[s][b] = (pool[s][b].astype(f32) - learn_rate * grad).astype(bf16)


def word_step(z, table, own, lanes, pool):
    return pl.pallas_call(
        functools.partial(word_kernel, z),
        out_shape=[jax.ShapeDtypeStruct((z.blocks, z.step, z.dim), bf16)] * z.half,
        in_specs=[SMEM] + [VMEM] * (2 + z.half),
        out_specs=[VMEM] * z.half,
        compiler_params=big,
        name="word_step",
    )(table, own, lanes, *pool)


def join_kernel(z, me_ref, *refs):
    pieces, out_ref, sem = refs[:-2], refs[-2], refs[-1]
    place = lax.rem(me_ref[1], z.half)
    copies = []
    for n, piece in enumerate(pieces):
        k, s = n // z.half, n % z.half
        row = pl.multiple_of((place ^ s) * z.part + k * z.step, 16)
        copies.append(pltpu.make_async_copy(piece, out_ref.at[:, pl.ds(row, z.step)], sem.at[n]))
    for copy in copies:
        copy.start()
    for copy in copies:
        copy.wait()


def join_words(z, me, pieces):
    return pl.pallas_call(
        functools.partial(join_kernel, z),
        out_shape=jax.ShapeDtypeStruct((z.blocks, z.block, z.dim), bf16),
        in_specs=[SMEM] + [ANY] * len(pieces),
        out_specs=VMEM,
        scratch_shapes=[pltpu.SemaphoreType.DMA((len(pieces),))],
        name="join_words",
    )(me, *pieces)


def give_kernel(z, info_ref, ctx_ref, *refs):
    out_ref, sem = refs[-2:]
    copies = []
    for p in range(z.rows):
        b = info_ref[8 + z.half + z.slots + p]
        copies.append(pltpu.make_async_copy(ctx_ref.at[b], out_ref.at[p], sem.at[p]))
    for copy in copies:
        copy.start()
    for copy in copies:
        copy.wait()


def give_contexts(z, info, contexts, after):
    return pl.pallas_call(
        functools.partial(give_kernel, z),
        out_shape=jax.ShapeDtypeStruct((z.rows, z.block, z.dim), bf16),
        in_specs=[SMEM, ANY] + [ANY] * len(after),
        out_specs=VMEM,
        scratch_shapes=[pltpu.SemaphoreType.DMA((z.rows,))],
        name="give_contexts",
    )(info, contexts, *after)


def context_kernel(z, info_ref, back_ref, ctx_ref, out_ref, total):
    total[...] = jnp.zeros_like(total)
    for p in range(z.rows):
        b = info_ref[8 + z.half + z.slots + p]
        total[b] = total[b] + back_ref[p].astype(f32)
    out_ref[...] = (ctx_ref[...].astype(f32) - learn_rate * total[...]).astype(bf16)


def context_step(z, info, back, contexts):
    n = z.block // 4
    return pl.pallas_call(
        functools.partial(context_kernel, z),
        out_shape=jax.ShapeDtypeStruct((z.blocks, z.block, z.dim), bf16),
        grid_spec=pltpu.PrefetchScalarGridSpec(
            num_scalar_prefetch=1,
            grid=(4,),
            in_specs=[
                pl.BlockSpec((z.rows, n, z.dim), lambda i, info: (0, i, 0)),
                pl.BlockSpec((z.blocks, n, z.dim), lambda i, info: (0, i, 0)),
            ],
            out_specs=pl.BlockSpec((z.blocks, n, z.dim), lambda i, info: (0, i, 0)),
            scratch_shapes=[pltpu.VMEM((z.blocks, n, z.dim), f32)],
        ),
        compiler_params=big,
        name="context_step",
    )(info, back, contexts)


def local(word_vecs, ctx_vecs, tile_rows, tile_cols, tile_count, counts, row_sums, col_sums):
    z = Sizes(word_vecs, counts)
    own_row, own_col = lax.axis_index("row"), lax.axis_index("col")
    place = own_col % z.half
    words = word_vecs[:, 0]
    contexts = ctx_vecs[:, 0]
    counts = counts[0, 0]
    row_sums = row_sums[0, 0].reshape(z.slots, z.half * chunks, 1, z.step)
    col_sums = col_sums[0, 0].reshape(z.slots, 1, z.block)
    me = jnp.stack([own_row, own_col]).astype(i32)

    def spread(k, after):
        pieces = split_words(z, k, me, words, after)
        return [pieces[0]] + [swap(pieces[s], "col", s) for s in range(1, z.half)]

    flat = tile_rows.reshape(1, z.cols * z.slots)
    lists = jnp.concatenate([flat] + [swap(flat, "row", s) for s in range(1, z.rows)])
    pool_0 = spread(0, [])
    table = make_table(z, me, lists, tile_count)

    col_lists = tile_cols[:, 0]
    mine = lax.dynamic_index_in_dim(col_lists, own_row, 0, False)
    live = tile_count[own_row, own_col]
    given = jnp.sum(jnp.where(col_lists // z.blocks == own_row, col_lists % z.blocks, 0), axis=1)
    info = jnp.concatenate(
        [
            jnp.full((8,), live, i32),
            place ^ jnp.arange(z.half, dtype=i32),
            mine // z.blocks,
            given,
        ]
    ).astype(i32)

    outgoing = give_contexts(z, info, contexts, [])

    def exchange(pieces):
        return [pieces[0]] + [swap(pieces[s], "col", s) for s in range(1, z.half)]

    def rest(cap):
        def run(pool_0, table, outgoing):
            ctx_tiles = lax.all_to_all(outgoing, "row", 0, 0, tiled=True)
            pools = [list(pool_0)] + [spread(k, []) for k in range(1, chunks)]
            so_far, lanes, asked, made, own, returned, pieces = None, [], [], [], [], [], []
            for k in range(chunks):
                lanes.append(across_col(pick_lanes(z, cap, table, pools[k], lanes[-1:])))
                order = []
                asked.append(pick_asked(z, cap, table, pools[k], lanes[k], order))
                *out, so_far = tile_step(
                    z, k, info, exchange(asked[k]), counts, row_sums, col_sums, ctx_tiles, so_far, []
                )
                made.append(out)
            for k in range(chunks):
                order = returned[-1:]
                sum_step(k, cap, table, exchange(made[k]), own, returned, order)
                pieces += exchange(word_step(z, table, own[k], returned[k], pools[k]))
            back = lax.all_to_all(so_far, "row", 0, 0, tiled=True)
            new_contexts = context_step(z, info, back, contexts)
            return join_words(z, me, pieces), new_contexts

        def sum_step(k, cap, table, parts, own, returned, after):
            total, grads = sum_parts(z, cap, table, parts, after)
            own.append(total)
            returned.append(across_col(grads))
            return [grads]

        return run

    def across_col(x):
        return swap(x, "col", z.half)

    caps = sorted({max(1, z.pool * n // 16) for n in (9, 16)})
    level = sum((table[0] > cap).astype(i32) for cap in caps[:-1])
    new_words, new_contexts = lax.switch(level, [rest(cap) for cap in caps], tuple(pool_0), table, outgoing)
    return new_words[:, None], new_contexts[:, None]


def solution(mesh):
    placed = (
        P("col", "row", None, None),
        P("row", "col", None, None),
        P("row", None, None),
        P(None, "col", None),
        P(),
        P("row", "col", None, None, None),
        P("row", "col", None, None),
        P("row", "col", None, None),
    )
    return jax.shard_map(
        local,
        mesh=mesh,
        in_specs=placed,
        out_specs=(P("col", "row", None, None), P("row", "col", None, None)),
        check_vma=False,
    )
```
